32 devices in a mesh: rows: 8 (over z, x), snap: 4 (over y, core).
Axes of the slice: x: 2, y: 2, z: 4, core: 2. Of those that a mesh axis runs over, the one named last changes fastest.
Arguments:
- snapshots: bfloat16 [12288, 1536], P('rows', 'snap'), may hold values from -6 to 6
- mass: bfloat16 [125, 12288], P(None, 'rows'), may hold values from -0.0048828125 to 0.0048828125
- counts: int32 [8], P('rows'), may hold values from 512 to 1536, as said below
- send_rows: int32 [8, 256], P('rows'), may hold values from 0 to 1535, as said below
- columns: int32 [125, 12288], P(None, 'rows'), may hold values from 0 to 1791, as said below
Outputs:
- gram_band: float32 [3, 1536, 384], P(None, ('snap', 'rows'))
The draws below stay inside these ranges and needn't reach their ends.
Inputs may be any that keep to these rules, and one draw needn't show every extreme that they name: counts[p] rows of partition p are live; some partition holds 1536 rows. send_rows[p, j] < counts[p]. `columns`: indices from 1536 on address the rows received from the left, then from the right neighbour.
All inputs are finite; a program needn't handle non-finite values.
Results may differ from the reference program's by a relative error of at most 0.003.
Values may be sent and summed in bfloat16 or wider, within the bound.
A program may use at most 64 MiB of HBM per device.

```python
import jax
import jax.numpy as jnp
from jax import lax

R_CAP = 1536
S_DEV = 384
HALO = 128
NNZ = 125
BAND = 3
PARTITIONS = 8
ROWS_ALL = 12288
SNAPS = 1536
N_SNAP = 4


def shared_counts(key):
    count_key = jax.random.fold_in(key, 11)
    drawn = jax.random.randint(count_key, (PARTITIONS,), R_CAP // 3, R_CAP + 1)
    fullest = jax.random.randint(jax.random.fold_in(key, 12), (), 0, PARTITIONS)
    places = jnp.arange(PARTITIONS)
    drawn = jnp.where(places == fullest, R_CAP, drawn)
    drawn = jnp.where(places == (fullest + 1) % PARTITIONS, R_CAP // 3, drawn)
    return drawn.astype(jnp.int32)


def draw_counts(key, part):
    drawn = shared_counts(key)
    return drawn


def draw_send_rows(key, part):
    row_counts = shared_counts(key)
    key = jax.random.fold_in(key, 2)
    drawn = jax.random.randint(key, (PARTITIONS, 2 * HALO), 0, 2 ** 30) % row_counts[:, None]
    slots = jnp.arange(2 * HALO)[None, :]
    drawn = jnp.where(slots == 0, row_counts[:, None] - 1, drawn)
    drawn = jnp.where(slots == 1, 0, drawn)
    return drawn.astype(jnp.int32)


def draw_columns(key, part):
    row_counts = shared_counts(key)
    key = jax.random.fold_in(key, 3)
    all_rows = jnp.arange(ROWS_ALL)
    owner = all_rows // R_CAP
    own_row = all_rows % R_CAP
    count_row = row_counts[owner][None, :]
    drawn = jax.random.randint(key, (NNZ, ROWS_ALL), 0, 2 ** 30) % (count_row + 2 * HALO)
    picked = jnp.where(drawn < count_row, drawn, drawn - count_row + R_CAP)
    entry = jnp.arange(NNZ)[:, None]
    picked = jnp.where(entry == 0, own_row[None, :], picked)
    picked = jnp.where((entry == 1) & (all_rows[None, :] == 0), R_CAP + 2 * HALO - 1, picked)
    return picked.astype(jnp.int32)


def levels(own_key, dims, cuts, smallest, top_value):
    def one(position, blocks):
        draws = jax.random.uniform(jax.random.fold_in(jax.random.fold_in(own_key, 6), position), (blocks,), jnp.float32, smallest / len(cuts), top_value / len(cuts))
        return jnp.repeat(jnp.exp(draws), dims[position] // blocks).reshape((-1,) + (1,) * (len(dims) - position - 1))

    factor_of = one(*cuts[0])
    for cut in cuts[1:]:
        factor_of = factor_of * one(*cut)
    return factor_of


def centred(rng, shape, deviation, most, cuts=(), kind=jnp.bfloat16):
    array = deviation * jax.random.normal(rng, shape, jnp.float32)
    if cuts:
        array = array * levels(rng, shape, cuts, -0.22, 0.18)
    return jnp.clip(array, -most, most).astype(kind)


def setup_inputs(seed: int = 0) -> dict:
    seeds = jax.random.split(jax.random.key(seed), 6)
    return {
        "snapshots": centred(seeds[0], (ROWS_ALL, SNAPS), 1.0, 6.0, ((0, 8), (1, 4))),
        "mass": centred(seeds[1], (NNZ, ROWS_ALL), (NNZ * ROWS_ALL) ** -0.5, 0.0048828125, ((1, 8),)),
        "counts": draw_counts(jax.random.fold_in(seeds[5], 71), 0),
        "send_rows": draw_send_rows(jax.random.fold_in(seeds[5], 71), 0),
        "columns": draw_columns(jax.random.fold_in(seeds[5], 71), 0),
    }


def reference(snapshots, mass, counts, send_rows, columns):
    blocks = snapshots.reshape(PARTITIONS, R_CAP, SNAPS)
    live_rows = jnp.arange(R_CAP)[None, :, None] < counts[:, None, None]
    masked = jnp.where(live_rows, blocks, jnp.zeros_like(blocks))
    outgoing = jax.vmap(lambda block, index: jnp.take(block, index, axis=0))(masked, send_rows)
    empty = jnp.zeros((1, HALO, SNAPS), masked.dtype)
    from_left = jnp.concatenate([empty, outgoing[:-1, HALO:]], 0)
    from_right = jnp.concatenate([outgoing[1:, :HALO], empty], 0)
    mass_parts = mass.reshape(NNZ, PARTITIONS, R_CAP).transpose(1, 0, 2)
    column_parts = columns.reshape(NNZ, PARTITIONS, R_CAP).transpose(1, 0, 2)
    row_index = jnp.broadcast_to(jnp.arange(R_CAP, dtype=jnp.int32)[None, :], (NNZ, R_CAP))

    def one_part(carry, inputs):
        block, left_rows, right_rows, weights, index, count = inputs
        extended = jnp.concatenate([block, left_rows, right_rows], 0)
        dense = jnp.zeros((R_CAP, R_CAP + 2 * HALO), jnp.float32)
        dense = dense.at[row_index, index].add(weights.astype(jnp.float32))
        operator = dense.astype(jnp.bfloat16)
        total = jnp.dot(operator, extended, preferred_element_type=jnp.float32)
        live = (jnp.arange(R_CAP) < count)[:, None]
        mass_image = jnp.where(live, total, jnp.zeros_like(total)).astype(jnp.bfloat16)
        left_blocks = block.astype(jnp.float32).reshape(R_CAP, N_SNAP, S_DEV)
        right_blocks = mass_image.astype(jnp.float32).reshape(R_CAP, N_SNAP, S_DEV)
        bands = jnp.stack([jnp.einsum("rns,rnt->nst", left_blocks, jnp.roll(right_blocks, offset, axis=1), precision=lax.Precision.HIGHEST) for offset in range(BAND)])
        return carry + bands, None

    start = jnp.zeros((BAND, N_SNAP, S_DEV, S_DEV), jnp.float32)
    total, unused = lax.scan(one_part, start, (masked, from_left, from_right, mass_parts, column_parts, counts))
    return total.reshape(BAND, SNAPS, S_DEV)
```

```python
import functools

import jax
import jax.numpy as jnp
from jax import lax
from jax.experimental import pallas as pl
from jax.experimental.pallas import tpu as pltpu
from jax.sharding import PartitionSpec as P

BAND = 3
LANES = 128
MESH = pl.DeviceIdType.MESH


def operator_kernel(cols_ref, mass_ref, op_ref, cols_pad, mass_pad, cols_t, mass_t, acc):
    nnz, tile = cols_ref.shape
    tiles = op_ref.shape[1] // LANES
    cols_pad[...] = jnp.zeros_like(cols_pad)
    mass_pad[...] = jnp.zeros_like(mass_pad)
    cols_pad[:nnz, :] = cols_ref[...]
    mass_pad[:nnz, :] = mass_ref[...].astype(jnp.float32)
    cols_t[...] = cols_pad[...].T
    mass_t[...] = mass_pad[...].T
    step = 16
    iota = lax.broadcasted_iota(jnp.int32, (LANES, LANES), 0).astype(jnp.float32).astype(jnp.bfloat16)
    iota_hi = iota[:16]
    zero = jnp.zeros((16, LANES), jnp.bfloat16)
    one = jnp.ones((LANES, LANES), jnp.bfloat16)
    zeros = jnp.zeros((LANES, LANES), jnp.bfloat16)

    def group(g, carry):
        base = pl.multiple_of(g * step, step)
        c = cols_t[pl.ds(base, step), :]
        low = (c & (LANES - 1)).astype(jnp.float32)
        high = (c // LANES).astype(jnp.float32)
        m = mass_t[pl.ds(base, step), :]
        for i in range(step):
            low_b = jnp.broadcast_to(low[i : i + 1], (16, LANES)).astype(jnp.bfloat16)
            high_b = jnp.broadcast_to(high[i : i + 1], (16, LANES)).astype(jnp.bfloat16)
            m_b = jnp.broadcast_to(m[i : i + 1], (16, LANES)).astype(jnp.bfloat16)
            left = jnp.where(high_b == iota_hi, m_b, zero)
            right = jnp.where(jnp.concatenate([low_b] * (LANES // 16), 0) == iota, one, zeros)
            out = lax.dot_general(left, right, (((1,), (1,)), ((), ())), preferred_element_type=jnp.float32)
            acc[pl.ds(pl.multiple_of(base * 16 + i * 16, 16), 16), :] = out
        return carry

    lax.fori_loop(0, tile // step, group, 0)
    for h in range(tiles):
        op_ref[:, h * LANES : (h + 1) * LANES] = acc[pl.ds(h, tile, stride=16), :].astype(op_ref.dtype)


def build_operator(columns, mass, width):
    nnz, rows_cap = columns.shape
    tile = LANES
    return pl.pallas_call(
        operator_kernel,
        grid=(rows_cap // tile,),
        out_shape=jax.ShapeDtypeStruct((rows_cap, width), jnp.bfloat16),
        in_specs=[pl.BlockSpec((nnz, tile), lambda i: (0, i))] * 2,
        out_specs=pl.BlockSpec((tile, width), lambda i: (i, 0)),
        scratch_shapes=[
            pltpu.VMEM((LANES, tile), jnp.int32),
            pltpu.VMEM((LANES, tile), jnp.float32),
            pltpu.VMEM((tile, LANES), jnp.int32),
            pltpu.VMEM((tile, LANES), jnp.float32),
            pltpu.VMEM((tile * 16, LANES), jnp.float32),
        ],
        compiler_params=pltpu.CompilerParams(vmem_limit_bytes=16 * 1024 * 1024),
        cost_estimate=pl.CostEstimate(flops=60_000_000_000, bytes_accessed=7_000_000, transcendentals=0),
    )(columns, mass)


def sum_kernel(parts, snaps, part_ref, out_ref, recv, stage, send_sem, recv_sem, shift_send, shift_recv):
    me = lax.axis_index("rows")
    here = lax.axis_index("snap")
    share = out_ref.shape[1]
    barrier = pltpu.get_barrier_semaphore()

    def greet(d, carry):
        pl.semaphore_signal(barrier, inc=1, device_id=(lax.rem(me + d, parts), here), device_id_type=MESH)
        return carry

    lax.fori_loop(1, parts, greet, 0)
    for k in range(1, BAND):
        pl.semaphore_signal(barrier, inc=1, device_id=(me, lax.rem(here + snaps - k, snaps)), device_id_type=MESH)
    pl.semaphore_wait(barrier, parts - 1 + BAND - 1)

    def copy(d):
        to = lax.rem(me + d, parts)
        return pltpu.make_async_remote_copy(
            src_ref=part_ref.at[to],
            dst_ref=recv.at[d],
            send_sem=send_sem.at[d],
            recv_sem=recv_sem.at[d],
            device_id=(to, here),
            device_id_type=MESH,
        )

    def start(d, carry):
        copy(d).start()
        return carry

    lax.fori_loop(1, parts, start, 0)

    def add(d, total):
        copy(d).wait_recv()
        return total + recv[d].astype(jnp.float32)

    stage[...] = lax.fori_loop(1, parts, add, part_ref[me].astype(jnp.float32))
    shifts = []
    for k in range(1, BAND):
        shift = pltpu.make_async_remote_copy(
            src_ref=stage.at[k],
            dst_ref=out_ref.at[k],
            send_sem=shift_send.at[k],
            recv_sem=shift_recv.at[k],
            device_id=(me, lax.rem(here + k, snaps)),
            device_id_type=MESH,
        )
        shift.start()
        shifts.append(shift)
    out_ref[0] = stage[0]

    def sent(d, carry):
        copy(d).wait_send()
        return carry

    lax.fori_loop(1, parts, sent, 0)
    for shift in shifts:
        shift.wait()


def sum_terms(terms, parts, snaps):
    share, width = terms.shape[2:]
    return pl.pallas_call(
        functools.partial(sum_kernel, parts, snaps),
        out_shape=jax.ShapeDtypeStruct((BAND, share, width), jnp.float32),
        in_specs=[pl.BlockSpec(memory_space=pltpu.VMEM)],
        out_specs=pl.BlockSpec(memory_space=pltpu.VMEM),
        scratch_shapes=[
            pltpu.VMEM(terms.shape, terms.dtype),
            pltpu.VMEM((BAND, share, width), jnp.float32),
            pltpu.SemaphoreType.DMA((parts,)),
            pltpu.SemaphoreType.DMA((parts,)),
            pltpu.SemaphoreType.DMA((BAND,)),
            pltpu.SemaphoreType.DMA((BAND,)),
        ],
        compiler_params=pltpu.CompilerParams(
            collective_id=0, has_side_effects=True, vmem_limit_bytes=24 * 1024 * 1024
        ),
    )(terms)


def shifted(value, axis, steps):
    count = lax.axis_size(axis)
    pairs = [(source, (source + steps) % count) for source in range(count)]
    return lax.ppermute(value, axis, pairs)


def band_term(masked, image):
    return lax.dot_general(masked, image, (((0,), (0,)), ((), ())), preferred_element_type=jnp.float32)


def body(snapshots, mass, counts, send_rows, columns):
    parts, snaps = lax.axis_size("rows"), lax.axis_size("snap")
    rows_cap, width = snapshots.shape
    halo_rows = send_rows.shape[1] // 2
    live_rows = lax.broadcasted_iota(jnp.int32, (rows_cap, 1), 0) < counts[0]
    masked = jnp.where(live_rows, snapshots, jnp.zeros_like(snapshots))
    outgoing = jnp.take(masked, send_rows[0], axis=0)
    up = [(i, i + 1) for i in range(parts - 1)]
    down = [(j, i) for i, j in up]
    from_left = lax.ppermute(outgoing[halo_rows:], "rows", up)
    from_right = lax.ppermute(outgoing[:halo_rows], "rows", down)
    lefts = [masked]
    for k in range(1, BAND):
        lefts.append(shifted(lefts[-1], "snap", -1))
    operator = build_operator(columns, mass, rows_cap + 2 * halo_rows)
    extended = jnp.concatenate([masked, from_left, from_right], 0)
    image = jnp.dot(operator, extended, preferred_element_type=jnp.float32)
    image = jnp.where(live_rows, image, jnp.zeros_like(image)).astype(jnp.bfloat16)
    terms = jnp.stack([band_term(left, image).reshape(parts, width // parts, width) for left in lefts], 1)
    return sum_terms(terms.astype(jnp.bfloat16), parts, snaps)


def solution(mesh):
    return jax.shard_map(
        body,
        mesh=mesh,
        in_specs=(P("rows", "snap"), P(None, "rows"), P("rows"), P("rows", None), P(None, "rows")),
        out_specs=P(None, ("snap", "rows"), None),
        check_vma=False,
    )
```

```python
import functools

import jax
import jax.numpy as jnp
from jax import lax
from jax.experimental import pallas as pl
from jax.experimental.pallas import tpu as pltpu
from jax.sharding import PartitionSpec as P

BAND = 3
LANES = 128
STEP = 16
MESH = pl.DeviceIdType.MESH
NT = (((1,), (1,)), ((), ()))
TN = (((0,), (0,)), ((), ()))


def operator_chunk(cols_ref, mass_ref, op_ref, start, cols_pad, mass_pad, cols_t, mass_t, acc):
    nnz = cols_ref.shape[0]
    tile = cols_t.shape[0]
    tiles = op_ref.shape[1] // LANES
    cols_pad[:nnz, :] = cols_ref[:, pl.ds(start, tile)]
    mass_pad[:nnz, :] = mass_ref[:, pl.ds(start, tile)].astype(jnp.float32)
    cols_t[...] = cols_pad[...].T
    mass_t[...] = mass_pad[...].T
    iota = lax.broadcasted_iota(jnp.int32, (LANES, LANES), 0).astype(jnp.float32).astype(jnp.bfloat16)
    zero = jnp.zeros((STEP, LANES), jnp.bfloat16)
    one = jnp.ones((LANES, LANES), jnp.bfloat16)
    zeros = jnp.zeros((LANES, LANES), jnp.bfloat16)

    def group(g, carry):
        base = pl.multiple_of(g * STEP, STEP)
        c = cols_t[pl.ds(base, STEP), :]
        low = (c & (LANES - 1)).astype(jnp.float32)
        high = (c >> 7).astype(jnp.float32)
        m = mass_t[pl.ds(base, STEP), :]

        def wide(x, i):
            return jnp.broadcast_to(x[i : i + 1], (16, LANES)).astype(jnp.bfloat16)

        def left(i):
            return jnp.where(wide(high, i) == iota[:16], wide(m, i), zero)

        def right(i):
            return jnp.where(jnp.concatenate([wide(low, i)] * (LANES // 16), 0) == iota, one, zeros)

        for i in range(0, STEP, 2):
            out = lax.dot_general(
                jnp.concatenate([left(i), left(i + 1)], 0),
                jnp.concatenate([right(i), right(i + 1)], 0),
                NT,
                preferred_element_type=jnp.float32,
            )
            at = pl.multiple_of(base * 16 + i * 16, 32)
            acc[pl.ds(at, 16), :] = out[:16, :LANES]
            acc[pl.ds(at + 16, 16), :] = out[16:, LANES:]
        return carry

    lax.fori_loop(0, tile // STEP, group, 0)
    for h in range(tiles):
        op_ref[pl.ds(start, tile), h * LANES : (h + 1) * LANES] = acc[pl.ds(h, tile, stride=16), :].astype(op_ref.dtype)


def kernel(
    parts, snaps, snap_ref, out_rows_ref, cols_ref, mass_ref, counts_ref, out_ref,
    ext, op, x1, x2, image, gram, terms, recv, stage,
    cols_pad, mass_pad, cols_t, mass_t, acc,
    halo_send, halo_recv, x_send, x_recv, op_send, op_recv, term_send, term_recv, shift_send, shift_recv,
):
    me = lax.axis_index("rows")
    here = lax.axis_index("snap")
    rows_cap, width = snap_ref.shape
    halo = out_rows_ref.shape[0] // 2
    share = out_ref.shape[1]
    half = rows_cap // 2
    tile = LANES
    chunks = half // tile
    count = counts_ref[0]
    odd = lax.rem(here, 2)
    mate = here + 1 - 2 * odd

    def remote(src, dst, send, arrive, row, snap):
        return pltpu.make_async_remote_copy(
            src_ref=src, dst_ref=dst, send_sem=send, recv_sem=arrive, device_id=(row, snap), device_id_type=MESH
        )

    barrier = pltpu.get_barrier_semaphore()

    def greet(d, carry):
        pl.semaphore_signal(barrier, inc=1, device_id=(lax.rem(me + d, parts), here), device_id_type=MESH)
        return carry

    lax.fori_loop(1, parts, greet, 0)
    offsets = sorted({k % snaps for k in (1, 2, -1, -2)})
    for k in offsets:
        pl.semaphore_signal(barrier, inc=1, device_id=(me, lax.rem(here + k, snaps)), device_id_type=MESH)
    pl.semaphore_wait(barrier, parts - 1 + len(offsets))

    def back(k):
        return lax.rem(here + snaps - k, snaps)

    first = remote(snap_ref, x1, x_send.at[0], x_recv.at[0], me, back(1))
    second = remote(snap_ref, x2, x_send.at[1], x_recv.at[1], me, back(2))
    relay = remote(x1, x2, x_send.at[2], x_recv.at[1], me, back(1))
    up = remote(
        out_rows_ref.at[pl.ds(halo, halo)], ext.at[pl.ds(rows_cap, halo)],
        halo_send.at[0], halo_recv.at[0], lax.rem(me + 1, parts), here,
    )
    down = remote(
        out_rows_ref.at[pl.ds(0, halo)], ext.at[pl.ds(rows_cap + halo, halo)],
        halo_send.at[1], halo_recv.at[1], lax.rem(me + parts - 1, parts), here,
    )
    up.start()
    down.start()
    first.start()

    @pl.when(odd == 1)
    def _():
        second.start()

    cols_pad[...] = jnp.zeros_like(cols_pad)
    mass_pad[...] = jnp.zeros_like(mass_pad)
    row = lax.broadcasted_iota(jnp.int32, (tile, width), 0)

    def mask(t, carry):
        at = pl.multiple_of(t * tile, tile)
        ext[pl.ds(at, tile), :] = jnp.where(row + at < count, snap_ref[pl.ds(at, tile), :].astype(jnp.float32), 0.0).astype(ext.dtype)
        return carry

    lax.fori_loop(0, rows_cap // tile, mask, 0)

    def lend(t):
        at = pl.multiple_of(odd * half + t * tile, tile)
        rows = op.at[pl.ds(at, tile)]
        return remote(rows, rows, op_send.at[t], op_recv.at[t], me, mate)

    def build(t, carry):
        at = pl.multiple_of(odd * half + t * tile, tile)
        operator_chunk(cols_ref, mass_ref, op, at, cols_pad, mass_pad, cols_t, mass_t, acc)
        lend(t).start()
        return carry

    lax.fori_loop(0, chunks, build, 0)

    up.wait()
    down.wait()

    @pl.when(me == 0)
    def _():
        ext[pl.ds(rows_cap, halo), :] = jnp.zeros((halo, width), ext.dtype)

    @pl.when(me == parts - 1)
    def _():
        ext[pl.ds(rows_cap + halo, halo), :] = jnp.zeros((halo, width), ext.dtype)

    big = 2 * tile
    row_big = lax.broadcasted_iota(jnp.int32, (big, width), 0)

    def multiply(at):
        value = jnp.dot(op[pl.ds(at, big), :], ext[...], preferred_element_type=jnp.float32)
        image[pl.ds(at, big), :] = jnp.where(row_big + at < count, value, 0.0).astype(image.dtype)

    def own(t, carry):
        multiply(pl.multiple_of(odd * half + t * big, big))
        return carry

    def lent(t, carry):
        lend(2 * t).wait_recv()
        lend(2 * t + 1).wait_recv()
        multiply(pl.multiple_of((1 - odd) * half + t * big, big))
        return carry

    lax.fori_loop(0, half // big, own, 0)
    lax.fori_loop(0, half // big, lent, 0)

    def term(k, d):
        to = lax.rem(me + d, parts)
        return remote(terms.at[k, to], recv.at[k, d], term_send.at[k, d], term_recv.at[k, d], to, here)

    def band(k, x_ref):
        gram[...] = lax.dot_general(x_ref[...], image[...], TN, preferred_element_type=jnp.float32)
        for q in range(parts):
            terms[k, q] = gram[q * share : (q + 1) * share, :].astype(terms.dtype)

        def start(d, carry):
            term(k, d).start()
            return carry

        lax.fori_loop(1, parts, start, 0)

    band(0, snap_ref)
    first.wait()

    @pl.when(odd == 1)
    def _():
        relay.start()

    band(1, x1)
    second.wait_recv()
    band(2, x2)

    def shift(k):
        return remote(stage.at[k], out_ref.at[k], shift_send.at[k], shift_recv.at[k], me, lax.rem(here + k, snaps))

    for k in range(BAND):

        def add(d, total):
            term(k, d).wait_recv()
            return total + recv[k, d].astype(jnp.float32)

        total = lax.fori_loop(1, parts, add, terms[k, me].astype(jnp.float32))
        if k == 0:
            out_ref[0] = total
        else:
            stage[k] = total
            shift(k).start()

    @pl.when(odd == 1)
    def _():
        second.wait_send()
        relay.wait_send()

    def lent_sent(t, carry):
        lend(t).wait_send()
        return carry

    lax.fori_loop(0, chunks, lent_sent, 0)

    def sent(d, carry):
        for k in range(BAND):
            term(k, d).wait_send()
        return carry

    lax.fori_loop(1, parts, sent, 0)
    for k in range(1, BAND):
        shift(k).wait()


def body(snapshots, mass, counts, send_rows, columns):
    parts, snaps = lax.axis_size("rows"), lax.axis_size("snap")
    rows_cap, width = snapshots.shape
    halo2 = send_rows.shape[1]
    share = width // parts
    wide = rows_cap + halo2
    chunks = rows_cap // 2 // LANES
    outgoing = jnp.take(snapshots, send_rows[0], axis=0)
    bf16, f32 = jnp.bfloat16, jnp.float32
    vmem = pl.BlockSpec(memory_space=pltpu.VMEM)
    return pl.pallas_call(
        functools.partial(kernel, parts, snaps),
        out_shape=jax.ShapeDtypeStruct((BAND, share, width), f32),
        in_specs=[vmem] * 4 + [pl.BlockSpec(memory_space=pltpu.SMEM)],
        out_specs=vmem,
        scratch_shapes=[
            pltpu.VMEM((wide, width), bf16),
            pltpu.VMEM((rows_cap, wide), bf16),
            pltpu.VMEM((rows_cap, width), bf16),
            pltpu.VMEM((rows_cap, width), bf16),
            pltpu.VMEM((rows_cap, width), bf16),
            pltpu.VMEM((width, width), f32),
            pltpu.VMEM((BAND, parts, share, width), bf16),
            pltpu.VMEM((BAND, parts, share, width), bf16),
            pltpu.VMEM((BAND, share, width), f32),
            pltpu.VMEM((LANES, LANES), jnp.int32),
            pltpu.VMEM((LANES, LANES), f32),
            pltpu.VMEM((LANES, LANES), jnp.int32),
            pltpu.VMEM((LANES, LANES), f32),
            pltpu.VMEM((LANES * 16, LANES), f32),
            pltpu.SemaphoreType.DMA((2,)),
            pltpu.SemaphoreType.DMA((2,)),
            pltpu.SemaphoreType.DMA((3,)),
            pltpu.SemaphoreType.DMA((2,)),
            pltpu.SemaphoreType.DMA((chunks,)),
            pltpu.SemaphoreType.DMA((chunks,)),
            pltpu.SemaphoreType.DMA((BAND, parts)),
            pltpu.SemaphoreType.DMA((BAND, parts)),
            pltpu.SemaphoreType.DMA((BAND,)),
            pltpu.SemaphoreType.DMA((BAND,)),
        ],
        compiler_params=pltpu.CompilerParams(
            collective_id=0, has_side_effects=True, vmem_limit_bytes=48 * 1024 * 1024
        ),
    )(snapshots, outgoing, columns, mass, counts)


def solution(mesh):
    return jax.shard_map(
        body,
        mesh=mesh,
        in_specs=(P("rows", "snap"), P(None, "rows"), P("rows"), P("rows", None), P(None, "rows")),
        out_specs=P(None, ("snap", "rows"), None),
        check_vma=False,
    )
```

```python
import functools

import jax
import jax.numpy as jnp
from jax import lax
from jax.experimental import pallas as pl
from jax.experimental.pallas import tpu as pltpu
from jax.sharding import PartitionSpec as P

BAND = 3
LANES = 128
STEP = 16
MESH = pl.DeviceIdType.MESH
NT = (((1,), (1,)), ((), ()))
TN = (((0,), (0,)), ((), ()))


def operator_chunk(cols_ref, mass_ref, op_ref, start, cols_pad, mass_pad, cols_t, mass_t, acc):
    nnz = cols_ref.shape[0]
    tile = cols_t.shape[0]
    tiles = op_ref.shape[1] // LANES
    cols_pad[:nnz, :] = cols_ref[:, pl.ds(start, tile)]
    mass_pad[:nnz, :] = mass_ref[:, pl.ds(start, tile)].astype(jnp.float32)
    cols_t[...] = cols_pad[...].T
    mass_t[...] = mass_pad[...].T
    iota = lax.broadcasted_iota(jnp.int32, (LANES, LANES), 0).astype(jnp.float32).astype(jnp.bfloat16)
    zero = jnp.zeros((STEP, LANES), jnp.bfloat16)
    one = jnp.ones((LANES, LANES), jnp.bfloat16)
    zeros = jnp.zeros((LANES, LANES), jnp.bfloat16)

    def group(g, carry):
        base = pl.multiple_of(g * STEP, STEP)
        c = cols_t[pl.ds(base, STEP), :]
        low = (c & (LANES - 1)).astype(jnp.float32)
        high = (c >> 7).astype(jnp.float32)
        m = mass_t[pl.ds(base, STEP), :]

        def wide(x, i):
            return jnp.broadcast_to(x[i : i + 1], (16, LANES)).astype(jnp.bfloat16)

        def left(i):
            return jnp.where(wide(high, i) == iota[:16], wide(m, i), zero)

        def right(i):
            return jnp.where(jnp.concatenate([wide(low, i)] * (LANES // 16), 0) == iota, one, zeros)

        for i in range(0, STEP, 2):
            out = lax.dot_general(
                jnp.concatenate([left(i), left(i + 1)], 0),
                jnp.concatenate([right(i), right(i + 1)], 0),
                NT,
                preferred_element_type=jnp.float32,
            )
            at = pl.multiple_of(base * 16 + i * 16, 32)
            acc[pl.ds(at, 16), :] = out[:16, :LANES]
            acc[pl.ds(at + 16, 16), :] = out[16:, LANES:]
        return carry

    lax.fori_loop(0, tile // STEP, group, 0)
    for h in range(tiles):
        op_ref[pl.ds(start, tile), h * LANES : (h + 1) * LANES] = acc[pl.ds(h, tile, stride=16), :].astype(op_ref.dtype)


def kernel(
    parts, snaps, snap_ref, send_ref, cols_ref, mass_ref, counts_ref, out_ref,
    outgoing, ext, op, x1, x2, image, gram, mine, theirs, visiting, pair, recv, recv_own,
    cols_pad, mass_pad, cols_t, mass_t, acc,
    halo_send, halo_recv, x_send, x_recv, op_send, op_recv,
    swap_send, swap_recv, term_send, term_recv, own_send, own_recv,
):
    me = lax.axis_index("rows")
    here = lax.axis_index("snap")
    rows_cap, width = snap_ref.shape
    halo = outgoing.shape[0] // 2
    share = out_ref.shape[1]
    half = rows_cap // 2
    tile = LANES
    chunks = half // tile
    groups = parts // 2
    count = counts_ref[0]
    odd = lax.rem(here, 2)
    mate = here + 1 - 2 * odd
    side = lax.rem(me, 2)
    group = lax.div(me, 2)
    partner = me + 1 - 2 * side
    after, before = lax.rem(me + 1, parts), lax.rem(me + parts - 1, parts)

    def remote(src, dst, send, arrive, row, snap):
        return pltpu.make_async_remote_copy(
            src_ref=src, dst_ref=dst, send_sem=send, recv_sem=arrive, device_id=(row, snap), device_id_type=MESH
        )

    def back(k):
        return lax.rem(here + snaps - k, snaps)

    def forward(k):
        return lax.rem(here + k, snaps)

    def member(d):
        return 2 * lax.rem(group + d, groups) + side

    barrier = pltpu.get_barrier_semaphore()

    def greet(row, snap):
        pl.semaphore_signal(barrier, inc=1, device_id=(row, snap), device_id_type=MESH)

    greet(after, here)
    greet(before, here)
    for k in range(1, BAND):
        greet(me, forward(k))
        greet(me, back(k))

    def greet_groups(d, carry):
        for k in range(BAND):
            greet(member(groups - d), back(k))
        return carry

    lax.fori_loop(1, groups, greet_groups, 0)
    pl.semaphore_wait(barrier, 2 + 2 * (BAND - 1) + BAND * (groups - 1))

    first = remote(snap_ref, x1, x_send.at[0], x_recv.at[0], me, back(1))
    second = remote(snap_ref, x2, x_send.at[1], x_recv.at[1], me, back(2))
    relay = remote(x1, x2, x_send.at[2], x_recv.at[1], me, back(1))
    up = remote(
        outgoing.at[pl.ds(halo, halo)], ext.at[pl.ds(rows_cap, halo)], halo_send.at[0], halo_recv.at[0], after, here
    )
    down = remote(
        outgoing.at[pl.ds(0, halo)], ext.at[pl.ds(rows_cap + halo, halo)], halo_send.at[1], halo_recv.at[1], before, here
    )
    first.start()

    own_half = pl.multiple_of(odd * half, tile)
    other_half = pl.multiple_of((1 - odd) * half, tile)
    wanted = jnp.broadcast_to(send_ref[...].astype(jnp.float32), (tile, 2 * halo)).T
    lane = lax.broadcasted_iota(jnp.int32, (2 * halo, tile), 1).astype(jnp.float32)
    picks = op.at[pl.ds(own_half, 2 * halo), pl.ds(0, rows_cap)]
    for t in range(rows_cap // tile):
        picks[:, t * tile : (t + 1) * tile] = jnp.where(wanted == lane + float(t * tile), 1.0, 0.0).astype(op.dtype)
    outgoing[...] = jnp.dot(picks[...], snap_ref[...], preferred_element_type=jnp.float32).astype(outgoing.dtype)
    up.start()
    down.start()

    cols_pad[...] = jnp.zeros_like(cols_pad)
    mass_pad[...] = jnp.zeros_like(mass_pad)
    row = lax.broadcasted_iota(jnp.int32, (tile, width), 0)

    def mask(t, carry):
        at = pl.multiple_of(t * tile, tile)
        block = snap_ref[pl.ds(at, tile), :].astype(jnp.float32)
        ext[pl.ds(at, tile), :] = jnp.where(row + at < count, block, 0.0).astype(ext.dtype)
        return carry

    lax.fori_loop(0, rows_cap // tile, mask, 0)

    def lend(t):
        rows = op.at[pl.ds(pl.multiple_of(own_half + t * tile, tile), tile)]
        return remote(rows, rows, op_send.at[t], op_recv.at[t], me, mate)

    def build(t, carry):
        at = pl.multiple_of(own_half + t * tile, tile)
        operator_chunk(cols_ref, mass_ref, op, at, cols_pad, mass_pad, cols_t, mass_t, acc)
        lend(t).start()
        return carry

    lax.fori_loop(0, chunks - 2, build, 0)

    @pl.when(odd == 1)
    def _():
        second.start()

    lax.fori_loop(chunks - 2, chunks - 1, build, 0)
    first.wait_recv()

    @pl.when(odd == 1)
    def _():
        relay.start()

    lax.fori_loop(chunks - 1, chunks, build, 0)

    up.wait()
    down.wait()

    @pl.when(me == 0)
    def _():
        ext[pl.ds(rows_cap, halo), :] = jnp.zeros((halo, width), ext.dtype)

    @pl.when(me == parts - 1)
    def _():
        ext[pl.ds(rows_cap + halo, halo), :] = jnp.zeros((halo, width), ext.dtype)

    big = 2 * tile
    row_big = lax.broadcasted_iota(jnp.int32, (big, width), 0)

    def multiply(at):
        value = jnp.dot(op[pl.ds(at, big), :], ext[...], preferred_element_type=jnp.float32)
        image[pl.ds(at, big), :] = jnp.where(row_big + at < count, value, 0.0).astype(image.dtype)

    def own(t, carry):
        multiply(pl.multiple_of(own_half + t * big, big))
        return carry

    def lent(t, carry):
        lend(2 * t).wait_recv()
        lend(2 * t + 1).wait_recv()
        multiply(pl.multiple_of(other_half + t * big, big))
        return carry

    lax.fori_loop(0, half // big, own, 0)
    lax.fori_loop(0, half // big, lent, 0)

    def swap(k):
        return remote(theirs.at[k], visiting.at[k], swap_send.at[k], swap_recv.at[k], partner, here)

    def term(k, d):
        to = lax.rem(group + d, groups)
        return remote(pair.at[k, to], recv.at[k, d], term_send.at[k, d], term_recv.at[k, d], 2 * to + side, forward(k))

    def own_share(k):
        return remote(mine.at[k, group], recv_own.at[k], own_send.at[k], own_recv.at[k], me, forward(k))

    def band(k, x_ref):
        gram[...] = lax.dot_general(x_ref[...], image[...], TN, preferred_element_type=jnp.float32)
        for g in range(groups):
            low = gram[2 * g * share : (2 * g + 1) * share, :]
            high = gram[(2 * g + 1) * share : (2 * g + 2) * share, :]
            mine[k, g] = jnp.where(side == 0, low, high)
            theirs[k, g] = jnp.where(side == 0, high, low).astype(theirs.dtype)
        swap(k).start()

    def spread(k):
        swap(k).wait_recv()
        for g in range(groups):
            total = mine[k, g] + visiting[k, g].astype(jnp.float32)
            mine[k, g] = total
            pair[k, g] = total.astype(pair.dtype)

        def start(d, carry):
            term(k, d).start()
            return carry

        lax.fori_loop(1, groups, start, 0)
        if k > 0:
            own_share(k).start()

    def collect(k):
        if k > 0:
            own_share(k).wait_recv()
            total = recv_own[k]
        else:
            total = mine[k, group]

        def add(d, total):
            term(k, d).wait_recv()
            return total + recv[k, d].astype(jnp.float32)

        out_ref[k] = lax.fori_loop(1, groups, add, total)

    band(0, snap_ref)
    band(1, x1)
    spread(0)
    second.wait_recv()
    band(2, x2)
    spread(1)
    spread(2)
    for k in range(BAND):
        collect(k)

    first.wait_send()

    @pl.when(odd == 1)
    def _():
        second.wait_send()
        relay.wait_send()

    def lent_sent(t, carry):
        lend(t).wait_send()
        return carry

    lax.fori_loop(0, chunks, lent_sent, 0)

    def sent(d, carry):
        for k in range(BAND):
            term(k, d).wait_send()
        return carry

    lax.fori_loop(1, groups, sent, 0)
    for k in range(BAND):
        swap(k).wait_send()
        if k > 0:
            own_share(k).wait_send()


def body(snapshots, mass, counts, send_rows, columns):
    parts, snaps = lax.axis_size("rows"), lax.axis_size("snap")
    rows_cap, width = snapshots.shape
    halo2 = send_rows.shape[1]
    share = width // parts
    groups = parts // 2
    wide = rows_cap + halo2
    chunks = rows_cap // 2 // LANES
    bf16, f32 = jnp.bfloat16, jnp.float32
    vmem = pl.BlockSpec(memory_space=pltpu.VMEM)
    dma = pltpu.SemaphoreType.DMA
    return pl.pallas_call(
        functools.partial(kernel, parts, snaps),
        out_shape=jax.ShapeDtypeStruct((BAND, share, width), f32),
        in_specs=[vmem] * 4 + [pl.BlockSpec(memory_space=pltpu.SMEM)],
        out_specs=vmem,
        scratch_shapes=[
            pltpu.VMEM((halo2, width), bf16),
            pltpu.VMEM((wide, width), bf16),
            pltpu.VMEM((rows_cap, wide), bf16),
            pltpu.VMEM((rows_cap, width), bf16),
            pltpu.VMEM((rows_cap, width), bf16),
            pltpu.VMEM((rows_cap, width), bf16),
            pltpu.VMEM((width, width), f32),
            pltpu.VMEM((BAND, groups, share, width), f32),
            pltpu.VMEM((BAND, groups, share, width), bf16),
            pltpu.VMEM((BAND, groups, share, width), bf16),
            pltpu.VMEM((BAND, groups, share, width), bf16),
            pltpu.VMEM((BAND, groups, share, width), bf16),
            pltpu.VMEM((BAND, share, width), f32),
            pltpu.VMEM((LANES, LANES), jnp.int32),
            pltpu.VMEM((LANES, LANES), f32),
            pltpu.VMEM((LANES, LANES), jnp.int32),
            pltpu.VMEM((LANES, LANES), f32),
            pltpu.VMEM((LANES * 16, LANES), f32),
            dma((2,)),
            dma((2,)),
            dma((3,)),
            dma((2,)),
            dma((chunks,)),
            dma((chunks,)),
            dma((BAND,)),
            dma((BAND,)),
            dma((BAND, groups)),
            dma((BAND, groups)),
            dma((BAND,)),
            dma((BAND,)),
        ],
        compiler_params=pltpu.CompilerParams(
            collective_id=0, has_side_effects=True, vmem_limit_bytes=48 * 1024 * 1024
        ),
    )(snapshots, send_rows, columns, mass, counts)


def solution(mesh):
    return jax.shard_map(
        body,
        mesh=mesh,
        in_specs=(P("rows", "snap"), P(None, "rows"), P("rows"), P("rows", None), P(None, "rows")),
        out_specs=P(None, ("snap", "rows"), None),
        check_vma=False,
    )
```

```python
import functools

import jax
import jax.numpy as jnp
from jax import lax
from jax.experimental import pallas as pl
from jax.experimental.pallas import tpu as pltpu
from jax.sharding import PartitionSpec as P

BAND = 3
LANES = 128
STEP = 16
MESH = pl.DeviceIdType.MESH
NT = (((1,), (1,)), ((), ()))
TN = (((0,), (0,)), ((), ()))


def operator_chunk(cols_ref, mass_ref, op_ref, start, cols_pad, mass_pad, cols_t, mass_t, acc):
    nnz = cols_ref.shape[0]
    tile = cols_t.shape[0]
    tiles = op_ref.shape[1] // LANES
    cols_pad[:nnz, :] = cols_ref[:, pl.ds(start, tile)]
    mass_pad[:nnz, :] = mass_ref[:, pl.ds(start, tile)].astype(jnp.float32)
    cols_t[...] = cols_pad[...].T
    mass_t[...] = mass_pad[...].T
    iota = lax.broadcasted_iota(jnp.int32, (LANES, LANES), 0).astype(jnp.float32).astype(jnp.bfloat16)
    zero = jnp.zeros((STEP, LANES), jnp.bfloat16)
    one = jnp.ones((LANES, LANES), jnp.bfloat16)
    zeros = jnp.zeros((LANES, LANES), jnp.bfloat16)

    def group(g, carry):
        base = pl.multiple_of(g * STEP, STEP)
        c = cols_t[pl.ds(base, STEP), :]
        low = (c & (LANES - 1)).astype(jnp.float32)
        high = (c >> 7).astype(jnp.float32)
        m = mass_t[pl.ds(base, STEP), :]

        def wide(x, i):
            return jnp.broadcast_to(x[i : i + 1], (16, LANES)).astype(jnp.bfloat16)

        def left(i):
            return jnp.where(wide(high, i) == iota[:16], wide(m, i), zero)

        def right(i):
            return jnp.where(jnp.concatenate([wide(low, i)] * (LANES // 16), 0) == iota, one, zeros)

        for i in range(0, STEP, 2):
            out = lax.dot_general(
                jnp.concatenate([left(i), left(i + 1)], 0),
                jnp.concatenate([right(i), right(i + 1)], 0),
                NT,
                preferred_element_type=jnp.float32,
            )
            at = pl.multiple_of(base * 16 + i * 16, 32)
            acc[pl.ds(at, 16), :] = out[:16, :LANES]
            acc[pl.ds(at + 16, 16), :] = out[16:, LANES:]
        return carry

    lax.fori_loop(0, tile // STEP, group, 0)
    for h in range(tiles):
        op_ref[pl.ds(start, tile), h * LANES : (h + 1) * LANES] = acc[pl.ds(h, tile, stride=16), :].astype(op_ref.dtype)


def kernel(
    parts, snaps, snap_hbm, send_ref, cols_hbm, mass_ref, counts_ref, out_ref,
    snap_ref, cols_ref, load_sem, outgoing, ext, op, x1, x2, image, gram, mine, theirs, visiting, pair, recv, recv_own,
    cols_pad, mass_pad, cols_t, mass_t, acc,
    halo_send, halo_recv, x_send, x_recv, op_send, op_recv,
    swap_send, swap_recv, term_send, term_recv, own_send, own_recv,
):
    load_snap = pltpu.make_async_copy(snap_hbm, snap_ref, load_sem.at[0])
    load_cols = pltpu.make_async_copy(cols_hbm, cols_ref, load_sem.at[1])
    load_snap.start()
    load_cols.start()
    me = lax.axis_index("rows")
    here = lax.axis_index("snap")
    rows_cap, width = snap_ref.shape
    halo = outgoing.shape[0] // 2
    share = out_ref.shape[1]
    half = rows_cap // 2
    tile = LANES
    chunks = half // tile
    groups = parts // 2
    count = counts_ref[0]
    odd = lax.rem(here, 2)
    mate = here + 1 - 2 * odd
    side = lax.rem(me, 2)
    group = lax.div(me, 2)
    partner = me + 1 - 2 * side
    after, before = lax.rem(me + 1, parts), lax.rem(me + parts - 1, parts)

    def remote(src, dst, send, arrive, row, snap):
        return pltpu.make_async_remote_copy(
            src_ref=src, dst_ref=dst, send_sem=send, recv_sem=arrive, device_id=(row, snap), device_id_type=MESH
        )

    def back(k):
        return lax.rem(here + snaps - k, snaps)

    def forward(k):
        return lax.rem(here + k, snaps)

    def member(d):
        return 2 * lax.rem(group + d, groups) + side

    barrier = pltpu.get_barrier_semaphore()

    def greet(row, snap):
        pl.semaphore_signal(barrier, inc=1, device_id=(row, snap), device_id_type=MESH)

    greet(after, here)
    greet(before, here)
    for k in range(1, BAND):
        greet(me, forward(k))
        greet(me, back(k))

    def greet_groups(d, carry):
        for k in range(BAND):
            greet(member(groups - d), back(k))
        return carry

    lax.fori_loop(1, groups, greet_groups, 0)
    pl.semaphore_wait(barrier, 2 + 2 * (BAND - 1) + BAND * (groups - 1))

    first = remote(snap_ref, x1, x_send.at[0], x_recv.at[0], me, back(1))
    second = remote(snap_ref, x2, x_send.at[1], x_recv.at[1], me, back(2))
    relay = remote(x1, x2, x_send.at[2], x_recv.at[1], me, back(1))
    up = remote(
        outgoing.at[pl.ds(halo, halo)], ext.at[pl.ds(rows_cap, halo)], halo_send.at[0], halo_recv.at[0], after, here
    )
    down = remote(
        outgoing.at[pl.ds(0, halo)], ext.at[pl.ds(rows_cap + halo, halo)], halo_send.at[1], halo_recv.at[1], before, here
    )
    load_snap.wait()
    first.start()

    own_half = pl.multiple_of(odd * half, tile)
    other_half = pl.multiple_of((1 - odd) * half, tile)
    wanted = jnp.broadcast_to(send_ref[...].astype(jnp.float32), (tile, 2 * halo)).T
    lane = lax.broadcasted_iota(jnp.int32, (2 * halo, tile), 1).astype(jnp.float32)
    picks = op.at[pl.ds(own_half, 2 * halo), pl.ds(0, rows_cap)]
    for t in range(rows_cap // tile):
        picks[:, t * tile : (t + 1) * tile] = jnp.where(wanted == lane + float(t * tile), 1.0, 0.0).astype(op.dtype)
    outgoing[...] = jnp.dot(picks[...], snap_ref[...], preferred_element_type=jnp.float32).astype(outgoing.dtype)
    up.start()
    down.start()

    load_cols.wait()
    cols_pad[...] = jnp.zeros_like(cols_pad)
    mass_pad[...] = jnp.zeros_like(mass_pad)
    row = lax.broadcasted_iota(jnp.int32, (tile, width), 0)

    def mask(t, carry):
        at = pl.multiple_of(t * tile, tile)
        block = snap_ref[pl.ds(at, tile), :].astype(jnp.float32)
        ext[pl.ds(at, tile), :] = jnp.where(row + at < count, block, 0.0).astype(ext.dtype)
        return carry

    lax.fori_loop(0, rows_cap // tile, mask, 0)

    def lend(t):
        rows = op.at[pl.ds(pl.multiple_of(own_half + t * tile, tile), tile)]
        return remote(rows, rows, op_send.at[t], op_recv.at[t], me, mate)

    def build(t, carry):
        at = pl.multiple_of(own_half + t * tile, tile)
        operator_chunk(cols_ref, mass_ref, op, at, cols_pad, mass_pad, cols_t, mass_t, acc)
        lend(t).start()
        return carry

    lax.fori_loop(0, chunks - 2, build, 0)

    @pl.when(odd == 1)
    def _():
        second.start()

    lax.fori_loop(chunks - 2, chunks, build, 0)
    first.wait_recv()

    @pl.when(odd == 1)
    def _():
        relay.start()

    up.wait()
    down.wait()

    @pl.when(me == 0)
    def _():
        ext[pl.ds(rows_cap, halo), :] = jnp.zeros((halo, width), ext.dtype)

    @pl.when(me == parts - 1)
    def _():
        ext[pl.ds(rows_cap + halo, halo), :] = jnp.zeros((halo, width), ext.dtype)

    big = 2 * tile
    row_big = lax.broadcasted_iota(jnp.int32, (big, width), 0)

    def multiply(at):
        value = jnp.dot(op[pl.ds(at, big), :], ext[...], preferred_element_type=jnp.float32)
        image[pl.ds(at, big), :] = jnp.where(row_big + at < count, value, 0.0).astype(image.dtype)

    def own(t, carry):
        multiply(pl.multiple_of(own_half + t * big, big))
        return carry

    def lent(t, carry):
        lend(2 * t).wait_recv()
        lend(2 * t + 1).wait_recv()
        multiply(pl.multiple_of(other_half + t * big, big))
        return carry

    lax.fori_loop(0, half // big, own, 0)
    lax.fori_loop(0, half // big, lent, 0)

    def swap(k):
        return remote(theirs.at[k], visiting.at[k], swap_send.at[k], swap_recv.at[k], partner, here)

    def term(k, d):
        to = lax.rem(group + d, groups)
        return remote(pair.at[k, to], recv.at[k, d], term_send.at[k, d], term_recv.at[k, d], 2 * to + side, forward(k))

    def own_share(k):
        return remote(mine.at[k, group], recv_own.at[k], own_send.at[k], own_recv.at[k], me, forward(k))

    def band(k, x_ref):
        gram[...] = lax.dot_general(x_ref[...], image[...], TN, preferred_element_type=jnp.float32)
        for g in range(groups):
            low = gram[2 * g * share : (2 * g + 1) * share, :]
            high = gram[(2 * g + 1) * share : (2 * g + 2) * share, :]
            mine[k, g] = jnp.where(side == 0, low, high)
            theirs[k, g] = jnp.where(side == 0, high, low).astype(theirs.dtype)
        swap(k).start()

    def spread(k):
        swap(k).wait_recv()
        for g in range(groups):
            total = mine[k, g] + visiting[k, g].astype(jnp.float32)
            mine[k, g] = total
            pair[k, g] = total.astype(pair.dtype)

        def start(d, carry):
            term(k, d).start()
            return carry

        lax.fori_loop(1, groups, start, 0)
        if k > 0:
            own_share(k).start()

    def collect(k):
        if k > 0:
            own_share(k).wait_recv()
            total = recv_own[k]
        else:
            total = mine[k, group]

        def add(d, total):
            term(k, d).wait_recv()
            return total + recv[k, d].astype(jnp.float32)

        out_ref[k] = lax.fori_loop(1, groups, add, total)

    band(0, snap_ref)
    band(1, x1)
    spread(0)
    second.wait_recv()
    band(2, x2)
    spread(1)
    spread(2)
    for k in range(BAND):
        collect(k)

    first.wait_send()

    @pl.when(odd == 1)
    def _():
        second.wait_send()
        relay.wait_send()

    def lent_sent(t, carry):
        lend(t).wait_send()
        return carry

    lax.fori_loop(0, chunks, lent_sent, 0)

    def sent(d, carry):
        for k in range(BAND):
            term(k, d).wait_send()
        return carry

    lax.fori_loop(1, groups, sent, 0)
    for k in range(BAND):
        swap(k).wait_send()
        if k > 0:
            own_share(k).wait_send()


def body(snapshots, mass, counts, send_rows, columns):
    parts, snaps = lax.axis_size("rows"), lax.axis_size("snap")
    rows_cap, width = snapshots.shape
    halo2 = send_rows.shape[1]
    share = width // parts
    groups = parts // 2
    wide = rows_cap + halo2
    chunks = rows_cap // 2 // LANES
    bf16, f32 = jnp.bfloat16, jnp.float32
    vmem = pl.BlockSpec(memory_space=pltpu.VMEM)
    hbm = pl.BlockSpec(memory_space=pltpu.HBM)
    dma = pltpu.SemaphoreType.DMA
    return pl.pallas_call(
        functools.partial(kernel, parts, snaps),
        out_shape=jax.ShapeDtypeStruct((BAND, share, width), f32),
        in_specs=[hbm, vmem, hbm, vmem, pl.BlockSpec(memory_space=pltpu.SMEM)],
        out_specs=vmem,
        scratch_shapes=[
            pltpu.VMEM(snapshots.shape, bf16),
            pltpu.VMEM(columns.shape, jnp.int32),
            dma((2,)),
            pltpu.VMEM((halo2, width), bf16),
            pltpu.VMEM((wide, width), bf16),
            pltpu.VMEM((rows_cap, wide), bf16),
            pltpu.VMEM((rows_cap, width), bf16),
            pltpu.VMEM((rows_cap, width), bf16),
            pltpu.VMEM((rows_cap, width), bf16),
            pltpu.VMEM((width, width), f32),
            pltpu.VMEM((BAND, groups, share, width), f32),
            pltpu.VMEM((BAND, groups, share, width), bf16),
            pltpu.VMEM((BAND, groups, share, width), bf16),
            pltpu.VMEM((BAND, groups, share, width), bf16),
            pltpu.VMEM((BAND, groups, share, width), bf16),
            pltpu.VMEM((BAND, share, width), f32),
            pltpu.VMEM((LANES, LANES), jnp.int32),
            pltpu.VMEM((LANES, LANES), f32),
            pltpu.VMEM((LANES, LANES), jnp.int32),
            pltpu.VMEM((LANES, LANES), f32),
            pltpu.VMEM((LANES * 16, LANES), f32),
            dma((2,)),
            dma((2,)),
            dma((3,)),
            dma((2,)),
            dma((chunks,)),
            dma((chunks,)),
            dma((BAND,)),
            dma((BAND,)),
            dma((BAND, groups)),
            dma((BAND, groups)),
            dma((BAND,)),
            dma((BAND,)),
        ],
        compiler_params=pltpu.CompilerParams(
            collective_id=0, has_side_effects=True, vmem_limit_bytes=62 * 1024 * 1024
        ),
    )(snapshots, send_rows, columns, mass, counts)


def solution(mesh):
    return jax.shard_map(
        body,
        mesh=mesh,
        in_specs=(P("rows", "snap"), P(None, "rows"), P("rows"), P("rows", None), P(None, "rows")),
        out_specs=P(None, ("snap", "rows"), None),
        check_vma=False,
    )
```
